32 devices in a mesh: surf: 4 (over y, x), norm: 8 (over z, core).
Axes of the slice: x: 2, y: 2, z: 4, core: 2. Of those that a mesh axis runs over, the one named last changes fastest.
Arguments:
- rhs: float32 [32, 48, 512], P('norm', None, 'surf'), may hold values from -6 to 6
- previous: float32 [32, 48, 512], P('norm', None, 'surf'), may hold values from -6 to 6
- minus_jac: bfloat16 [32, 48, 48, 512], P('norm', None, None, 'surf'), may hold values from -0.4375 to 0.4375
- plus_jac: bfloat16 [32, 48, 48, 512], P('norm', None, None, 'surf'), may hold values from -0.4375 to 0.4375
- dissipation: float32 [32, 48, 512], P('norm', None, 'surf'), may hold values from 0.01 to 0.08
- inverse_diag: bfloat16 [32, 48, 48, 512], P('norm', None, None, 'surf'), may hold values from -0.15625 to 0.15625
- lower_coupling: bfloat16 [32, 48, 48, 512], P('norm', None, None, 'surf'), may hold values from -0.1484375 to 1, as said below
- upper_coupling: bfloat16 [32, 48, 48, 512], P('norm', None, None, 'surf'), may hold values from -0.1484375 to 1, as said below
Outputs:
- update: float32 [32, 48, 512], P('norm', None, 'surf')
The draws below stay inside these ranges and needn't reach their ends.
Inputs may be any that keep to these rules, and one draw needn't show every extreme that they name: `lower_coupling`: diagonal entries in (0, 1], off-diagonal entries small. `upper_coupling`: diagonal entries in (0, 1], off-diagonal entries small.
All inputs are finite; a program needn't handle non-finite values.
Results may differ from the reference program's by a relative error of at most 0.0003.
Values may be sent and summed in bfloat16 or wider, within the bound.
A program may use at most 512 MiB of HBM per device.

```python
import math
import jax
import jax.numpy as jnp
from jax import lax

NEQ = 48
SWEEPS = 2
NS = 512
NORMAL_CELLS = 32


def coupling(key, low, high):
    random_key_list = jax.random.split(key, 3)
    unit_matrix = jnp.eye(NEQ, dtype=jnp.float32)[None, :, :, None]
    damping_rates = jnp.exp(jax.random.uniform(random_key_list[0], (1, NEQ, 1, NS), minval=math.log(low), maxval=math.log(high)))
    source_pulses = jnp.where(jax.random.uniform(random_key_list[1], (NORMAL_CELLS, 1, 1, 1)) < 3.0 / NORMAL_CELLS, 0.6, 1.0)
    species_blending = jnp.clip(0.03 * jax.random.normal(random_key_list[2], (NORMAL_CELLS, NEQ, NEQ, NS)), -0.1484375, 0.1484375)
    cell_block_set = unit_matrix * jnp.exp(-damping_rates / NORMAL_CELLS) * source_pulses + species_blending * (1.0 - unit_matrix)
    return cell_block_set.astype(jnp.bfloat16)


def draw_lower_coupling(key, part):
    key = jax.random.fold_in(key, 11)
    return coupling(key, 0.5, 24.0)


def draw_upper_coupling(key, part):
    key = jax.random.fold_in(key, 23)
    return coupling(key, 0.5, 24.0)


def steps_of(own_key, extent, cuts, smallest, high):
    loudness, own = 1.0, jax.random.fold_in(own_key, 6)
    for dim, parts in cuts:
        steps = jnp.exp(jax.random.uniform(jax.random.fold_in(own, dim), (parts,), jnp.float32, smallest / len(cuts), high / len(cuts)))
        loudness = loudness * jnp.repeat(steps, extent[dim] // parts).reshape([-1 if axis == dim else 1 for axis in range(len(extent))])
    return loudness


def centred(key, shape, deviation, most, shards=(), kind=jnp.bfloat16):
    loudness = steps_of(key, shape, shards, -0.22, 0.18) if shards else 1.0
    result = jax.random.normal(key, shape, jnp.float32) * deviation * loudness
    return jnp.minimum(jnp.maximum(result, -most), most).astype(kind)


def setup_inputs(seed: int = 0) -> dict:
    key_of = jax.random.split(jax.random.key(seed), 9)
    return {
        "rhs": centred(key_of[0], (NORMAL_CELLS, NEQ, NS), 1.0, 6.0, ((0, 8), (2, 4)), jnp.float32),
        "previous": centred(key_of[1], (NORMAL_CELLS, NEQ, NS), 1.0, 6.0, ((0, 8), (2, 4)), jnp.float32),
        "minus_jac": centred(key_of[2], (NORMAL_CELLS, NEQ, NEQ, NS), (4 * NEQ) ** -0.5, 0.4375, ((0, 8), (3, 4))),
        "plus_jac": centred(key_of[3], (NORMAL_CELLS, NEQ, NEQ, NS), (4 * NEQ) ** -0.5, 0.4375, ((0, 8), (3, 4))),
        "dissipation": jnp.clip(jnp.exp(math.log(0.08) - 2.0794415 * jax.random.uniform(key_of[4], (NORMAL_CELLS, NEQ, NS), jnp.float32) ** steps_of(key_of[4], (NORMAL_CELLS, NEQ, NS), ((0, 8), (2, 4)), -0.2, 0.2)), 0.01, 0.08),
        "inverse_diag": centred(key_of[5], (NORMAL_CELLS, NEQ, NEQ, NS), (NEQ * NORMAL_CELLS) ** -0.5, 0.15625, ((0, 8), (3, 4))),
        "lower_coupling": draw_lower_coupling(jax.random.fold_in(key_of[8], 71), 0),
        "upper_coupling": draw_upper_coupling(jax.random.fold_in(key_of[8], 71), 0),
    }


HIGH = lax.Precision.HIGHEST


def matvec(block, vector):
    return jnp.einsum('abs,bs->as', block.astype(jnp.float32), vector, precision=HIGH)


def reference(rhs, previous, minus_jac, plus_jac, dissipation, inverse_diag, lower_coupling, upper_coupling):
    delta = previous
    width = rhs.shape[2]
    for sweep_index in range(SWEEPS):
        padded = jnp.pad(delta, ((0, 0), (0, 0), (2, 2)))
        left_two = padded[:, :, 0:width]
        left_one = padded[:, :, 1:width + 1]
        centre = padded[:, :, 2:width + 2]
        right_one = padded[:, :, 3:width + 3]
        right_two = padded[:, :, 4:width + 4]
        fourth = left_two - 4.0 * left_one + 6.0 * centre - 4.0 * right_one + right_two

        def per_cell(items):
            residual_cell, below, above, minus_block, plus_block, inverse_block = items
            return matvec(inverse_block, residual_cell - matvec(minus_block, below) - matvec(plus_block, above))

        source = lax.map(per_cell, (rhs - dissipation * fourth, left_one, right_one, minus_jac, plus_jac, inverse_diag))

        def advance(carry, items):
            source_cell, block = items
            value = source_cell + matvec(block, carry)
            return value, value

        start = jnp.zeros(rhs.shape[1:], jnp.float32)
        forward_last, forward_values = lax.scan(advance, start, (source, lower_coupling))
        backward_first, backward_values = lax.scan(advance, start, (forward_values, upper_coupling), reverse=True)
        delta = backward_values
    return delta
```

```python
import functools

import jax
import jax.numpy as jnp
from jax import lax
from jax.experimental import pallas as pl
from jax.experimental.pallas import tpu as pltpu
from jax.sharding import PartitionSpec as P

SWEEPS = 2
ROWS = 8
EDGE = 2
F32 = jnp.float32


def row_sums(regs):
    row = lax.broadcasted_iota(jnp.int32, regs[0].shape, 0)
    for half in (4, 2, 1):
        low = (row % (2 * half)) < half
        merged = []
        for i in range(half):
            a, b = regs[i], regs[i + half]
            keep = jnp.where(low, a, b)
            move = jnp.where(low, b, a)
            if half == 4:
                moved = pltpu.roll(move, half, 0)
            else:
                moved = jnp.where(
                    low, pltpu.roll(move, ROWS - half, 0), pltpu.roll(move, half, 0)
                )
            merged.append(keep + moved)
        regs = merged
    return regs[0]


def matvec(block_ref, cell, vector):
    equations = vector.shape[0]
    out = []
    for group in range(equations // ROWS):
        regs = []
        for a in range(ROWS):
            product = block_ref[cell, group * ROWS + a].astype(F32) * vector
            parts = [product[i : i + ROWS] for i in range(0, equations, ROWS)]
            while len(parts) > 1:
                parts = [
                    parts[i] + parts[i + 1] if i + 1 < len(parts) else parts[i]
                    for i in range(0, len(parts), 2)
                ]
            regs.append(parts[0])
        out.append(row_sums(regs))
    return jnp.concatenate(out, axis=0)


def pack_edges(cell):
    equations, width = cell.shape
    lane = lax.broadcasted_iota(jnp.int32, (ROWS, width), 1)
    packed = jnp.zeros((ROWS, width), F32)
    for g in range(equations // ROWS):
        moved = pltpu.roll(cell[g * ROWS : (g + 1) * ROWS], EDGE + 2 * EDGE * g, 1)
        packed = jnp.where(lane // (2 * EDGE) == g, moved, packed)
    return packed


def unpack_edges(packed, equations):
    width = packed.shape[1]
    return jnp.concatenate(
        [
            pltpu.roll(packed, width - EDGE - 2 * EDGE * g, 1)
            for g in range(equations // ROWS)
        ],
        axis=0,
    )


def kernel(
    rhs_h, prev_h, minus_h, plus_h, diss_h, inv_h, low_h, up_h, out_h,
    rhs, delta, minus, plus, diss, inv, low, up, source, line,
    edge_out, edge_in, carry_out, carry_in,
    load_sem, block_sem, store_sem, edge_send, edge_recv, carry_send, carry_recv,
):
    cells, equations, width = rhs.shape
    norm, surf = lax.axis_index("norm"), lax.axis_index("surf")
    norms, surfs = lax.axis_size("norm"), lax.axis_size("surf")
    has_below, has_above = norm > 0, norm < norms - 1
    has_left, has_right = surf > 0, surf < surfs - 1

    small = [
        pltpu.make_async_copy(src, dst, load_sem.at[i])
        for i, (src, dst) in enumerate(((prev_h, delta), (rhs_h, rhs), (diss_h, diss)))
    ]
    pairs = ((minus_h, minus), (plus_h, plus), (inv_h, inv), (low_h, low), (up_h, up))

    def block_copy(kind, cell):
        src, dst = pairs[kind]
        return pltpu.make_async_copy(src.at[cell], dst.at[cell], block_sem.at[kind, cell])

    for copy in small:
        copy.start()
    for cell in range(cells):
        for kind in range(3):
            block_copy(kind, cell).start()
    for cell in range(cells):
        block_copy(3, cell).start()
    for cell in reversed(range(cells)):
        block_copy(4, cell).start()

    neighbours = (
        (has_below, {"norm": norm - 1}),
        (has_above, {"norm": norm + 1}),
        (has_left, {"surf": surf - 1}),
        (has_right, {"surf": surf + 1}),
    )
    barrier = pltpu.get_barrier_semaphore()
    for present, where in neighbours:
        @pl.when(present)
        def _():
            pl.semaphore_signal(
                barrier, inc=1, device_id=where, device_id_type=pl.DeviceIdType.MESH
            )

    @pl.when(jnp.logical_not(has_left))
    def _():
        edge_in[:, 0] = jnp.zeros_like(edge_in[:, 0])

    @pl.when(jnp.logical_not(has_right))
    def _():
        edge_in[:, 1] = jnp.zeros_like(edge_in[:, 1])

    @pl.when(jnp.logical_not(has_below))
    def _():
        for sweep in range(SWEEPS):
            carry_in[2 * sweep] = jnp.zeros((equations, width), F32)

    @pl.when(jnp.logical_not(has_above))
    def _():
        for sweep in range(SWEEPS):
            carry_in[2 * sweep + 1] = jnp.zeros((equations, width), F32)

    pl.semaphore_wait(barrier, sum(present.astype(jnp.int32) for present, _ in neighbours))

    def edge_copy(sweep, side, cell):
        return pltpu.make_async_remote_copy(
            src_ref=edge_out.at[sweep, cell],
            dst_ref=edge_in.at[sweep, side, cell],
            send_sem=edge_send.at[sweep, side, cell],
            recv_sem=edge_recv.at[sweep, side, cell],
            device_id={"surf": surf + 1 - 2 * side},
            device_id_type=pl.DeviceIdType.MESH,
        )

    def carry_copy(index):
        return pltpu.make_async_remote_copy(
            src_ref=carry_out.at[index],
            dst_ref=carry_in.at[index],
            send_sem=carry_send.at[index],
            recv_sem=carry_recv.at[index],
            device_id={"norm": norm + 1 - 2 * (index % 2)},
            device_id_type=pl.DeviceIdType.MESH,
        )

    def send_edges(sweep, cell, value):
        edge_out[sweep, cell] = pack_edges(value)

        @pl.when(has_right)
        def _():
            edge_copy(sweep, 0, cell).start()

        @pl.when(has_left)
        def _():
            edge_copy(sweep, 1, cell).start()

    lane = lax.broadcasted_iota(jnp.int32, (equations, width), 1)

    def source_cell(sweep, cell):
        @pl.when(has_left)
        def _():
            edge_copy(sweep, 0, cell).wait_recv()

        @pl.when(has_right)
        def _():
            edge_copy(sweep, 1, cell).wait_recv()

        if sweep == 0:
            for kind in range(3):
                block_copy(kind, cell).wait()
        centre = delta[cell]
        left = unpack_edges(edge_in[sweep, 0, cell], equations)
        right = unpack_edges(edge_in[sweep, 1, cell], equations)
        left_one = pltpu.roll(jnp.where(lane == width - 1, left, centre), 1, 1)
        left_two = pltpu.roll(jnp.where(lane >= width - 2, left, centre), 2, 1)
        right_one = pltpu.roll(jnp.where(lane == 0, right, centre), width - 1, 1)
        right_two = pltpu.roll(jnp.where(lane <= 1, right, centre), width - 2, 1)
        fourth = left_two - 4.0 * left_one + 6.0 * centre - 4.0 * right_one + right_two
        residual = rhs[cell] - diss[cell] * fourth
        residual = residual - matvec(minus, cell, left_one)
        residual = residual - matvec(plus, cell, right_one)
        source[cell] = matvec(inv, cell, residual)

    small[0].wait()

    def first_edges(cell, _):
        send_edges(0, cell, delta[cell])
        return 0

    lax.fori_loop(0, cells, first_edges, 0)
    small[1].wait()
    small[2].wait()

    for sweep in range(SWEEPS):
        last_sweep = sweep == SWEEPS - 1

        def source_step(step, _):
            source_cell(sweep, step if sweep == 0 else cells - 1 - step)
            return 0

        lax.fori_loop(0, cells, source_step, 0)

        def forward_step(cell, carry):
            value = source[cell] + matvec(low, cell, carry)
            line[cell] = value
            return value

        def backward_step(step, carry):
            cell = cells - 1 - step
            value = line[cell] + matvec(up, cell, carry)
            delta[cell] = value
            if last_sweep:
                pltpu.make_async_copy(delta.at[cell], out_h.at[cell], store_sem.at[cell]).start()
            else:
                send_edges(sweep + 1, cell, value)
            return value

        for index, step, arrives, leaves, kind in (
            (2 * sweep, forward_step, has_below, has_above, 3),
            (2 * sweep + 1, backward_step, has_above, has_below, 4),
        ):
            if sweep == 0:
                for cell in range(cells):
                    block_copy(kind, cell).wait()

            @pl.when(arrives)
            def _():
                carry_copy(index).wait_recv()

            carry = lax.fori_loop(0, cells, step, carry_in[index])

            @pl.when(leaves)
            def _():
                carry_out[index] = carry
                carry_copy(index).start()

    for cell in range(cells):
        pltpu.make_async_copy(delta.at[cell], out_h.at[cell], store_sem.at[cell]).wait()
    for sweep in range(SWEEPS):
        for cell in range(cells):
            for side, present in ((0, has_right), (1, has_left)):
                @pl.when(present)
                def _():
                    edge_copy(sweep, side, cell).wait_send()

        for index, leaves in ((2 * sweep, has_above), (2 * sweep + 1, has_below)):
            @pl.when(leaves)
            def _():
                carry_copy(index).wait_send()


def shards(*arrays):
    cells, equations, width = arrays[0].shape
    vector = pltpu.VMEM((cells, equations, width), F32)
    matrix = pltpu.VMEM((cells, equations, equations, width), jnp.bfloat16)
    dma = pltpu.SemaphoreType.DMA
    return pl.pallas_call(
        kernel,
        out_shape=jax.ShapeDtypeStruct((cells, equations, width), F32),
        in_specs=[pl.BlockSpec(memory_space=pl.ANY)] * len(arrays),
        out_specs=pl.BlockSpec(memory_space=pl.ANY),
        scratch_shapes=[
            vector, vector, matrix, matrix, vector, matrix, matrix, matrix, vector, vector,
            pltpu.VMEM((SWEEPS, cells, ROWS, width), F32),
            pltpu.VMEM((SWEEPS, 2, cells, ROWS, width), F32),
            pltpu.VMEM((2 * SWEEPS, equations, width), F32),
            pltpu.VMEM((2 * SWEEPS, equations, width), F32),
            dma((3,)), dma((5, cells)), dma((cells,)),
            dma((SWEEPS, 2, cells)), dma((SWEEPS, 2, cells)),
            dma((2 * SWEEPS,)), dma((2 * SWEEPS,)),
        ],
        compiler_params=pltpu.CompilerParams(
            collective_id=0, has_side_effects=True, vmem_limit_bytes=56 * 1024 * 1024
        ),
        name="line_relaxation",
    )(*arrays)


def solution(mesh):
    vectors = P("norm", None, "surf")
    blocks = P("norm", None, None, "surf")
    return jax.shard_map(
        shards,
        mesh=mesh,
        in_specs=(vectors, vectors, blocks, blocks, vectors, blocks, blocks, blocks),
        out_specs=vectors,
        check_vma=False,
    )
```

```python
import functools

import jax
import jax.numpy as jnp
from jax import lax
from jax.experimental import pallas as pl
from jax.experimental.pallas import tpu as pltpu
from jax.sharding import PartitionSpec as P

SWEEPS = 2
ROWS = 8
EDGE = 2
CHUNK = 16
F32 = jnp.float32


def row_sums(regs):
    row = lax.broadcasted_iota(jnp.int32, regs[0].shape, 0)
    for half in (4, 2, 1):
        low = (row % (2 * half)) < half
        merged = []
        for i in range(half):
            a, b = regs[i], regs[i + half]
            keep = jnp.where(low, a, b)
            move = jnp.where(low, b, a)
            if half == 4:
                moved = pltpu.roll(move, half, 0)
            else:
                moved = jnp.where(
                    low, pltpu.roll(move, ROWS - half, 0), pltpu.roll(move, half, 0)
                )
            merged.append(keep + moved)
        regs = merged
    return regs[0]


def matvec(block_ref, cell, vector, each_group=None):
    equations = vector.shape[0]
    out = []
    for group in range(equations // ROWS):
        regs = []
        for a in range(ROWS):
            product = block_ref[cell, group * ROWS + a].astype(F32) * vector
            parts = [product[i : i + ROWS] for i in range(0, equations, ROWS)]
            while len(parts) > 1:
                parts = [
                    parts[i] + parts[i + 1] if i + 1 < len(parts) else parts[i]
                    for i in range(0, len(parts), 2)
                ]
            regs.append(parts[0])
        out.append(row_sums(regs))
        if each_group is not None:
            each_group(group, out[-1])
    return jnp.concatenate(out, axis=0)


def pack_edges(cell):
    equations, width = cell.shape
    lane = lax.broadcasted_iota(jnp.int32, (ROWS, width), 1)
    packed = jnp.zeros((ROWS, width), F32)
    for g in range(equations // ROWS):
        moved = pltpu.roll(cell[g * ROWS : (g + 1) * ROWS], EDGE + 2 * EDGE * g, 1)
        packed = jnp.where(lane // (2 * EDGE) == g, moved, packed)
    return packed


def unpack_edges(packed, equations):
    width = packed.shape[1]
    return jnp.concatenate(
        [
            pltpu.roll(packed, width - EDGE - 2 * EDGE * g, 1)
            for g in range(equations // ROWS)
        ],
        axis=0,
    )


def kernel(
    rhs_h, prev_h, minus_h, plus_h, diss_h, inv_h, low_h, up_h, out_h,
    rhs, delta, minus, plus, diss, inv, low, up, source, line,
    edge_out, edge_in, carry_out, carry_in, low_wide, up_wide,
    load_sem, block_sem, store_sem, edge_send, edge_recv, carry_send, carry_recv,
):
    cells, equations, width = rhs.shape
    norm, surf = lax.axis_index("norm"), lax.axis_index("surf")
    norms, surfs = lax.axis_size("norm"), lax.axis_size("surf")
    has_below, has_above = norm > 0, norm < norms - 1
    has_left, has_right = surf > 0, surf < surfs - 1

    small = [
        pltpu.make_async_copy(src, dst, load_sem.at[i])
        for i, (src, dst) in enumerate(((prev_h, delta), (rhs_h, rhs), (diss_h, diss)))
    ]
    pairs = ((minus_h, minus), (plus_h, plus), (inv_h, inv), (low_h, low), (up_h, up))

    def block_copy(kind, cell):
        src, dst = pairs[kind]
        return pltpu.make_async_copy(src.at[cell], dst.at[cell], block_sem.at[kind, cell])

    for copy in small:
        copy.start()
    for cell in range(cells):
        for kind in range(3):
            block_copy(kind, cell).start()
    for cell in range(cells):
        block_copy(3, cell).start()
    for cell in reversed(range(cells)):
        block_copy(4, cell).start()

    neighbours = (
        (has_below, {"norm": norm - 1}),
        (has_above, {"norm": norm + 1}),
        (has_left, {"surf": surf - 1}),
        (has_right, {"surf": surf + 1}),
    )
    barrier = pltpu.get_barrier_semaphore()
    for present, where in neighbours:
        @pl.when(present)
        def _():
            pl.semaphore_signal(
                barrier, inc=1, device_id=where, device_id_type=pl.DeviceIdType.MESH
            )

    @pl.when(jnp.logical_not(has_left))
    def _():
        edge_in[:, 0] = jnp.zeros_like(edge_in[:, 0])

    @pl.when(jnp.logical_not(has_right))
    def _():
        edge_in[:, 1] = jnp.zeros_like(edge_in[:, 1])

    pl.semaphore_wait(barrier, sum(present.astype(jnp.int32) for present, _ in neighbours))

    def edge_copy(sweep, side, cell):
        return pltpu.make_async_remote_copy(
            src_ref=edge_out.at[sweep, cell],
            dst_ref=edge_in.at[sweep, side, cell],
            send_sem=edge_send.at[sweep, side, cell],
            recv_sem=edge_recv.at[sweep, side, cell],
            device_id={"surf": surf + 1 - 2 * side},
            device_id_type=pl.DeviceIdType.MESH,
        )

    def carry_copy(index, chunk):
        rows = pl.ds(chunk * CHUNK, CHUNK)
        return pltpu.make_async_remote_copy(
            src_ref=carry_out.at[index, rows],
            dst_ref=carry_in.at[index, rows],
            send_sem=carry_send.at[index, chunk],
            recv_sem=carry_recv.at[index, chunk],
            device_id={"norm": norm + 1 - 2 * (index % 2)},
            device_id_type=pl.DeviceIdType.MESH,
        )

    def widen(kind, wide):
        def rows(step, _):
            cell, group = step // (equations // ROWS), step % (equations // ROWS)
            for a in range(ROWS):
                row = group * ROWS + a
                wide[cell, row] = pairs[kind][1][cell, row].astype(F32)
            return 0

        for cell in range(cells):
            block_copy(kind, cell).wait()
        lax.fori_loop(0, cells * (equations // ROWS), rows, 0)

    def send_edges(sweep, cell, value):
        edge_out[sweep, cell] = pack_edges(value)

        @pl.when(has_right)
        def _():
            edge_copy(sweep, 0, cell).start()

        @pl.when(has_left)
        def _():
            edge_copy(sweep, 1, cell).start()

    lane = lax.broadcasted_iota(jnp.int32, (equations, width), 1)

    def source_cell(sweep, cell):
        @pl.when(has_left)
        def _():
            edge_copy(sweep, 0, cell).wait_recv()

        @pl.when(has_right)
        def _():
            edge_copy(sweep, 1, cell).wait_recv()

        if sweep == 0:
            for kind in range(3):
                block_copy(kind, cell).wait()
        centre = delta[cell]
        left = unpack_edges(edge_in[sweep, 0, cell], equations)
        right = unpack_edges(edge_in[sweep, 1, cell], equations)
        left_one = pltpu.roll(jnp.where(lane == width - 1, left, centre), 1, 1)
        left_two = pltpu.roll(jnp.where(lane >= width - 2, left, centre), 2, 1)
        right_one = pltpu.roll(jnp.where(lane == 0, right, centre), width - 1, 1)
        right_two = pltpu.roll(jnp.where(lane <= 1, right, centre), width - 2, 1)
        fourth = left_two - 4.0 * left_one + 6.0 * centre - 4.0 * right_one + right_two
        residual = rhs[cell] - diss[cell] * fourth
        residual = residual - matvec(minus, cell, left_one)
        residual = residual - matvec(plus, cell, right_one)
        source[cell] = matvec(inv, cell, residual)

    small[0].wait()

    def first_edges(cell, _):
        send_edges(0, cell, delta[cell])
        return 0

    lax.fori_loop(0, cells, first_edges, 0)
    small[1].wait()
    small[2].wait()

    for sweep in range(SWEEPS):
        last_sweep = sweep == SWEEPS - 1

        def source_step(step, _):
            source_cell(sweep, step if sweep == 0 else cells - 1 - step)
            return 0

        lax.fori_loop(0, cells, source_step, 0)

        def run_pass(index, arrives, leaves, blocks, given, result, finish):
            backward = index % 2
            place = lambda step: cells - 1 - step if backward else step

            @pl.when(arrives)
            def _():
                for chunk in range(equations // CHUNK):
                    carry_copy(index, chunk).wait_recv()

            @pl.when(jnp.logical_not(arrives))
            def _():
                first = given[place(0)]
                carry_in[index] = first
                result[place(0)] = first
                finish(place(0), first)

            def step_cell(step, carry):
                cell = place(step)
                value = given[cell] + matvec(blocks, cell, carry)
                result[cell] = value
                finish(cell, value)
                return value

            begin = 1 - arrives.astype(jnp.int32)
            carry = lax.fori_loop(begin, cells - 1, step_cell, carry_in[index])
            last = place(cells - 1)

            @pl.when(leaves)
            def _():
                def send_group(group, sums):
                    rows = slice(group * ROWS, (group + 1) * ROWS)
                    carry_out[index, rows] = given[last, rows] + sums
                    if (group + 1) * ROWS % CHUNK == 0:
                        carry_copy(index, group * ROWS // CHUNK).start()

                matvec(blocks, last, carry, send_group)
                value = carry_out[index]
                result[last] = value
                finish(last, value)

            @pl.when(jnp.logical_not(leaves))
            def _():
                value = given[last] + matvec(blocks, last, carry)
                result[last] = value
                finish(last, value)

        def keep(cell, value):
            pass

        def pass_on(cell, value):
            if last_sweep:
                pltpu.make_async_copy(delta.at[cell], out_h.at[cell], store_sem.at[cell]).start()
            else:
                send_edges(sweep + 1, cell, value)

        if sweep == 0:
            widen(3, low_wide)

            @pl.when(has_below)
            def _():
                widen(4, up_wide)

        run_pass(2 * sweep, has_below, has_above, low_wide, source, line, keep)
        if sweep == 0:
            @pl.when(jnp.logical_not(has_below))
            def _():
                widen(4, up_wide)

        run_pass(2 * sweep + 1, has_above, has_below, up_wide, line, delta, pass_on)

    for cell in range(cells):
        pltpu.make_async_copy(delta.at[cell], out_h.at[cell], store_sem.at[cell]).wait()
    for sweep in range(SWEEPS):
        for cell in range(cells):
            for side, present in ((0, has_right), (1, has_left)):
                @pl.when(present)
                def _():
                    edge_copy(sweep, side, cell).wait_send()

        for index, leaves in ((2 * sweep, has_above), (2 * sweep + 1, has_below)):
            @pl.when(leaves)
            def _():
                for chunk in range(equations // CHUNK):
                    carry_copy(index, chunk).wait_send()


def shards(*arrays):
    cells, equations, width = arrays[0].shape
    vector = pltpu.VMEM((cells, equations, width), F32)
    matrix = pltpu.VMEM((cells, equations, equations, width), jnp.bfloat16)
    wide = pltpu.VMEM((cells, equations, equations, width), F32)
    dma = pltpu.SemaphoreType.DMA
    return pl.pallas_call(
        kernel,
        out_shape=jax.ShapeDtypeStruct((cells, equations, width), F32),
        in_specs=[pl.BlockSpec(memory_space=pl.ANY)] * len(arrays),
        out_specs=pl.BlockSpec(memory_space=pl.ANY),
        scratch_shapes=[
            vector, vector, matrix, matrix, vector, matrix, matrix, matrix, vector, vector,
            pltpu.VMEM((SWEEPS, cells, ROWS, width), F32),
            pltpu.VMEM((SWEEPS, 2, cells, ROWS, width), F32),
            pltpu.VMEM((2 * SWEEPS, equations, width), F32),
            pltpu.VMEM((2 * SWEEPS, equations, width), F32),
            wide, wide,
            dma((3,)), dma((5, cells)), dma((cells,)),
            dma((SWEEPS, 2, cells)), dma((SWEEPS, 2, cells)),
            dma((2 * SWEEPS, equations // CHUNK)), dma((2 * SWEEPS, equations // CHUNK)),
        ],
        compiler_params=pltpu.CompilerParams(
            collective_id=0, has_side_effects=True, vmem_limit_bytes=56 * 1024 * 1024
        ),
        name="line_relaxation",
    )(*arrays)


def solution(mesh):
    vectors = P("norm", None, "surf")
    blocks = P("norm", None, None, "surf")
    return jax.shard_map(
        shards,
        mesh=mesh,
        in_specs=(vectors, vectors, blocks, blocks, vectors, blocks, blocks, blocks),
        out_specs=vectors,
        check_vma=False,
    )
```

```python
import functools

import jax
import jax.numpy as jnp
from jax import lax
from jax.experimental import pallas as pl
from jax.experimental.pallas import tpu as pltpu
from jax.sharding import PartitionSpec as P

SWEEPS = 2
ROWS = 8
EDGE = 2
CHUNK = 16
TILE = 4
F32 = jnp.float32


def row_sums(regs):
    row = lax.broadcasted_iota(jnp.int32, regs[0].shape, 0)
    for half in (4, 2, 1):
        low = (row % (2 * half)) < half
        merged = []
        for i in range(half):
            a, b = regs[i], regs[i + half]
            keep = jnp.where(low, a, b)
            move = jnp.where(low, b, a)
            if half == 4:
                moved = pltpu.roll(move, half, 0)
            else:
                moved = jnp.where(
                    low, pltpu.roll(move, ROWS - half, 0), pltpu.roll(move, half, 0)
                )
            merged.append(keep + moved)
        regs = merged
    return regs[0]


def matvec(block_ref, cell, vector, each_group=None):
    equations = vector.shape[0]
    out = []
    for group in range(equations // ROWS):
        regs = []
        for a in range(ROWS):
            product = block_ref[cell, group * ROWS + a].astype(F32) * vector
            parts = [product[i : i + ROWS] for i in range(0, equations, ROWS)]
            while len(parts) > 1:
                parts = [
                    parts[i] + parts[i + 1] if i + 1 < len(parts) else parts[i]
                    for i in range(0, len(parts), 2)
                ]
            regs.append(parts[0])
        out.append(row_sums(regs))
        if each_group is not None:
            each_group(group, out[-1])
    return jnp.concatenate(out, axis=0)


def pack_edges(cell):
    equations, width = cell.shape
    lane = lax.broadcasted_iota(jnp.int32, (ROWS, width), 1)
    packed = jnp.zeros((ROWS, width), F32)
    for g in range(equations // ROWS):
        moved = pltpu.roll(cell[g * ROWS : (g + 1) * ROWS], EDGE + 2 * EDGE * g, 1)
        packed = jnp.where(lane // (2 * EDGE) == g, moved, packed)
    return packed


def unpack_edges(packed, equations):
    width = packed.shape[1]
    return jnp.concatenate(
        [
            pltpu.roll(packed, width - EDGE - 2 * EDGE * g, 1)
            for g in range(equations // ROWS)
        ],
        axis=0,
    )


def kernel(
    rhs_h, prev_h, minus_h, plus_h, diss_h, inv_h, low_h, up_h, out_h,
    rhs, delta, minus, plus, diss, inv, low, up, source, line,
    edge_out, edge_in, carry_out, carry_in, wide, joined, local_out,
    load_sem, block_sem, store_sem, edge_send, edge_recv, carry_send, carry_recv,
):
    cells, equations, width = rhs.shape
    norm, surf = lax.axis_index("norm"), lax.axis_index("surf")
    norms, surfs = lax.axis_size("norm"), lax.axis_size("surf")
    has_below, has_above = norm > 0, norm < norms - 1
    has_left, has_right = surf > 0, surf < surfs - 1

    small = [
        pltpu.make_async_copy(src, dst, load_sem.at[i])
        for i, (src, dst) in enumerate(((prev_h, delta), (rhs_h, rhs), (diss_h, diss)))
    ]
    pairs = ((minus_h, minus), (plus_h, plus), (inv_h, inv), (low_h, low), (up_h, up))

    def block_copy(kind, cell):
        src, dst = pairs[kind]
        return pltpu.make_async_copy(src.at[cell], dst.at[cell], block_sem.at[kind, cell])

    for copy in small:
        copy.start()
    for cell in range(cells):
        for kind in range(3):
            block_copy(kind, cell).start()
    for cell in range(cells):
        block_copy(3, cell).start()
    for cell in reversed(range(cells)):
        block_copy(4, cell).start()

    neighbours = (
        (has_below, {"norm": norm - 1}),
        (has_above, {"norm": norm + 1}),
        (has_left, {"surf": surf - 1}),
        (has_right, {"surf": surf + 1}),
    )
    barrier = pltpu.get_barrier_semaphore()
    for present, where in neighbours:
        @pl.when(present)
        def _():
            pl.semaphore_signal(
                barrier, inc=1, device_id=where, device_id_type=pl.DeviceIdType.MESH
            )

    @pl.when(jnp.logical_not(has_left))
    def _():
        edge_in[:, 0] = jnp.zeros_like(edge_in[:, 0])

    @pl.when(jnp.logical_not(has_right))
    def _():
        edge_in[:, 1] = jnp.zeros_like(edge_in[:, 1])

    pl.semaphore_wait(barrier, sum(present.astype(jnp.int32) for present, _ in neighbours))

    def edge_copy(sweep, side, cell):
        return pltpu.make_async_remote_copy(
            src_ref=edge_out.at[sweep, cell],
            dst_ref=edge_in.at[sweep, side, cell],
            send_sem=edge_send.at[sweep, side, cell],
            recv_sem=edge_recv.at[sweep, side, cell],
            device_id={"surf": surf + 1 - 2 * side},
            device_id_type=pl.DeviceIdType.MESH,
        )

    def carry_copy(index, chunk):
        rows = pl.ds(chunk * CHUNK, CHUNK)
        return pltpu.make_async_remote_copy(
            src_ref=carry_out.at[index, rows],
            dst_ref=carry_in.at[index, rows],
            send_sem=carry_send.at[index, chunk],
            recv_sem=carry_recv.at[index, chunk],
            device_id={"norm": norm + 1 - 2 * (index % 2)},
            device_id_type=pl.DeviceIdType.MESH,
        )

    def widen(kind):
        def rows(step, _):
            cell, group = step // (equations // ROWS), step % (equations // ROWS)
            for a in range(ROWS):
                row = group * ROWS + a
                wide[kind - 3, cell, row] = pairs[kind][1][cell, row].astype(F32)
            return 0

        for cell in range(cells):
            block_copy(kind, cell).wait()
        lax.fori_loop(0, cells * (equations // ROWS), rows, 0)

    def join(unit, _):
        kind, step = unit // (cells - 1), unit % (cells - 1)
        cell = (step + 1) * (1 - kind) + (cells - 2 - step) * kind
        made, used = step % 2, (step + 1) % 2

        @pl.when(step == 0)
        def _():
            def copy_row(row, _):
                joined[kind, 1, row] = wide[kind, (cells - 1) * kind, row]
                return 0

            lax.fori_loop(0, equations, copy_row, 0)

        def rows(group, _):
            tile = pl.ds(group * TILE, TILE)
            total = jnp.zeros((TILE, equations, width), F32)
            for b in range(equations):
                total += wide[kind, cell, tile, b : b + 1, :] * joined[kind, used, b][None]
            joined[kind, made, tile] = total
            return 0

        lax.fori_loop(0, equations // TILE, rows, 0)
        return 0

    units = 2 * (cells - 1)
    early_units = jnp.minimum(units, norms - 1 - norm)

    def send_edges(sweep, cell, value):
        edge_out[sweep, cell] = pack_edges(value)

        @pl.when(has_right)
        def _():
            edge_copy(sweep, 0, cell).start()

        @pl.when(has_left)
        def _():
            edge_copy(sweep, 1, cell).start()

    lane = lax.broadcasted_iota(jnp.int32, (equations, width), 1)

    def source_cell(sweep, cell):
        @pl.when(has_left)
        def _():
            edge_copy(sweep, 0, cell).wait_recv()

        @pl.when(has_right)
        def _():
            edge_copy(sweep, 1, cell).wait_recv()

        if sweep == 0:
            for kind in range(3):
                block_copy(kind, cell).wait()
        centre = delta[cell]
        left = unpack_edges(edge_in[sweep, 0, cell], equations)
        right = unpack_edges(edge_in[sweep, 1, cell], equations)
        left_one = pltpu.roll(jnp.where(lane == width - 1, left, centre), 1, 1)
        left_two = pltpu.roll(jnp.where(lane >= width - 2, left, centre), 2, 1)
        right_one = pltpu.roll(jnp.where(lane == 0, right, centre), width - 1, 1)
        right_two = pltpu.roll(jnp.where(lane <= 1, right, centre), width - 2, 1)
        fourth = left_two - 4.0 * left_one + 6.0 * centre - 4.0 * right_one + right_two
        residual = rhs[cell] - diss[cell] * fourth
        residual = residual - matvec(minus, cell, left_one)
        residual = residual - matvec(plus, cell, right_one)
        source[cell] = matvec(inv, cell, residual)

    small[0].wait()

    def first_edges(cell, _):
        send_edges(0, cell, delta[cell])
        return 0

    lax.fori_loop(0, cells, first_edges, 0)
    small[1].wait()
    small[2].wait()

    for sweep in range(SWEEPS):
        last_sweep = sweep == SWEEPS - 1

        def source_step(step, _):
            source_cell(sweep, step if sweep == 0 else cells - 1 - step)
            return 0

        lax.fori_loop(0, cells, source_step, 0)

        def run_pass(index, arrives, leaves, blocks, given, result, finish):
            backward = index % 2
            place = lambda step: cells - 1 - step if backward else step

            @pl.when(arrives)
            def _():
                for chunk in range(equations // CHUNK):
                    carry_copy(index, chunk).wait_recv()

            @pl.when(jnp.logical_not(arrives))
            def _():
                first = given[place(0)]
                carry_in[index] = first
                result[place(0)] = first
                finish(place(0), first)

            def step_cell(step, carry):
                cell = place(step)
                value = given[cell] + matvec(blocks, cell, carry)
                result[cell] = value
                finish(cell, value)
                return value

            begin = 1 - arrives.astype(jnp.int32)
            carry = lax.fori_loop(begin, cells - 1, step_cell, carry_in[index])
            last = place(cells - 1)

            @pl.when(leaves)
            def _():
                def send_group(group, sums):
                    rows = slice(group * ROWS, (group + 1) * ROWS)
                    carry_out[index, rows] = given[last, rows] + sums
                    if (group + 1) * ROWS % CHUNK == 0:
                        carry_copy(index, group * ROWS // CHUNK).start()

                matvec(blocks, last, carry, send_group)
                value = carry_out[index]
                result[last] = value
                finish(last, value)

            @pl.when(jnp.logical_not(leaves))
            def _():
                value = given[last] + matvec(blocks, last, carry)
                result[last] = value
                finish(last, value)

        def run_joined(index, arrives, leaves, blocks, given, result, finish):
            backward = index % 2
            place = lambda step: cells - 1 - step if backward else step
            middle = jnp.logical_and(arrives, leaves)
            last = place(cells - 1)

            @pl.when(middle)
            def _():
                def local_step(step, carry):
                    cell = place(step)
                    return given[cell] + matvec(blocks, cell, carry)

                local_out[...] = lax.fori_loop(1, cells, local_step, given[place(0)])
                for chunk in range(equations // CHUNK):
                    carry_copy(index, chunk).wait_recv()

                def send_group(group, sums):
                    rows = slice(group * ROWS, (group + 1) * ROWS)
                    carry_out[index, rows] = local_out[rows] + sums
                    if (group + 1) * ROWS % CHUNK == 0:
                        carry_copy(index, group * ROWS // CHUNK).start()

                matvec(joined.at[backward], cells % 2, carry_in[index], send_group)

                def step_cell(step, carry):
                    cell = place(step)
                    value = given[cell] + matvec(blocks, cell, carry)
                    result[cell] = value
                    finish(cell, value)
                    return value

                lax.fori_loop(0, cells - 1, step_cell, carry_in[index])
                value = carry_out[index]
                result[last] = value
                finish(last, value)

            @pl.when(jnp.logical_not(middle))
            def _():
                run_pass(index, arrives, leaves, blocks, given, result, finish)

        def keep(cell, value):
            pass

        def pass_on(cell, value):
            if last_sweep:
                pltpu.make_async_copy(delta.at[cell], out_h.at[cell], store_sem.at[cell]).start()
            else:
                send_edges(sweep + 1, cell, value)

        if sweep == 0:
            widen(3)

            @pl.when(has_below)
            def _():
                widen(4)

        run = run_pass if sweep == 0 else run_joined
        if sweep == 1:
            lax.fori_loop(early_units, units, join, 0)
        run(2 * sweep, has_below, has_above, wide.at[0], source, line, keep)
        if sweep == 0:
            @pl.when(jnp.logical_not(has_below))
            def _():
                widen(4)

            lax.fori_loop(0, early_units, join, 0)

        run(2 * sweep + 1, has_above, has_below, wide.at[1], line, delta, pass_on)

    for cell in range(cells):
        pltpu.make_async_copy(delta.at[cell], out_h.at[cell], store_sem.at[cell]).wait()
    for sweep in range(SWEEPS):
        for cell in range(cells):
            for side, present in ((0, has_right), (1, has_left)):
                @pl.when(present)
                def _():
                    edge_copy(sweep, side, cell).wait_send()

        for index, leaves in ((2 * sweep, has_above), (2 * sweep + 1, has_below)):
            @pl.when(leaves)
            def _():
                for chunk in range(equations // CHUNK):
                    carry_copy(index, chunk).wait_send()


def shards(*arrays):
    cells, equations, width = arrays[0].shape
    vector = pltpu.VMEM((cells, equations, width), F32)
    matrix = pltpu.VMEM((cells, equations, equations, width), jnp.bfloat16)
    dma = pltpu.SemaphoreType.DMA
    return pl.pallas_call(
        kernel,
        out_shape=jax.ShapeDtypeStruct((cells, equations, width), F32),
        in_specs=[pl.BlockSpec(memory_space=pl.ANY)] * len(arrays),
        out_specs=pl.BlockSpec(memory_space=pl.ANY),
        scratch_shapes=[
            vector, vector, matrix, matrix, vector, matrix, matrix, matrix, vector, vector,
            pltpu.VMEM((SWEEPS, cells, ROWS, width), F32),
            pltpu.VMEM((SWEEPS, 2, cells, ROWS, width), F32),
            pltpu.VMEM((2 * SWEEPS, equations, width), F32),
            pltpu.VMEM((2 * SWEEPS, equations, width), F32),
            pltpu.VMEM((2, cells, equations, equations, width), F32),
            pltpu.VMEM((2, 2, equations, equations, width), F32),
            pltpu.VMEM((equations, width), F32),
            dma((3,)), dma((5, cells)), dma((cells,)),
            dma((SWEEPS, 2, cells)), dma((SWEEPS, 2, cells)),
            dma((2 * SWEEPS, equations // CHUNK)), dma((2 * SWEEPS, equations // CHUNK)),
        ],
        compiler_params=pltpu.CompilerParams(
            collective_id=0, has_side_effects=True, vmem_limit_bytes=56 * 1024 * 1024
        ),
        name="line_relaxation",
    )(*arrays)


def solution(mesh):
    vectors = P("norm", None, "surf")
    blocks = P("norm", None, None, "surf")
    return jax.shard_map(
        shards,
        mesh=mesh,
        in_specs=(vectors, vectors, blocks, blocks, vectors, blocks, blocks, blocks),
        out_specs=vectors,
        check_vma=False,
    )
```

```python
import functools

import jax
import jax.numpy as jnp
from jax import lax
from jax.experimental import pallas as pl
from jax.experimental.pallas import tpu as pltpu
from jax.sharding import PartitionSpec as P

SWEEPS = 2
ROWS = 8
EDGE = 2
CHUNK = 16
TILE = 4
F32 = jnp.float32


def row_sums(regs):
    row = lax.broadcasted_iota(jnp.int32, regs[0].shape, 0)
    for half in (4, 2, 1):
        low = (row % (2 * half)) < half
        merged = []
        for i in range(half):
            a, b = regs[i], regs[i + half]
            keep = jnp.where(low, a, b)
            move = jnp.where(low, b, a)
            if half == 4:
                moved = pltpu.roll(move, half, 0)
            else:
                moved = jnp.where(
                    low, pltpu.roll(move, ROWS - half, 0), pltpu.roll(move, half, 0)
                )
            merged.append(keep + moved)
        regs = merged
    return regs[0]


def matvec(block_ref, cell, vector, each_group=None):
    equations = vector.shape[0]
    out = []
    for group in range(equations // ROWS):
        regs = []
        for a in range(ROWS):
            product = block_ref[cell, group * ROWS + a].astype(F32) * vector
            parts = [product[i : i + ROWS] for i in range(0, equations, ROWS)]
            while len(parts) > 1:
                parts = [
                    parts[i] + parts[i + 1] if i + 1 < len(parts) else parts[i]
                    for i in range(0, len(parts), 2)
                ]
            regs.append(parts[0])
        out.append(row_sums(regs))
        if each_group is not None:
            each_group(group, out[-1])
    return jnp.concatenate(out, axis=0)


def pack_edges(cell):
    equations, width = cell.shape
    lane = lax.broadcasted_iota(jnp.int32, (ROWS, width), 1)
    packed = jnp.zeros((ROWS, width), F32)
    for g in range(equations // ROWS):
        moved = pltpu.roll(cell[g * ROWS : (g + 1) * ROWS], EDGE + 2 * EDGE * g, 1)
        packed = jnp.where(lane // (2 * EDGE) == g, moved, packed)
    return packed


def unpack_edges(packed, equations):
    width = packed.shape[1]
    return jnp.concatenate(
        [
            pltpu.roll(packed, width - EDGE - 2 * EDGE * g, 1)
            for g in range(equations // ROWS)
        ],
        axis=0,
    )


def kernel(
    rhs_h, prev_h, minus_h, plus_h, diss_h, inv_h, low_h, up_h, out_h,
    rhs, delta, minus, plus, diss, inv, low, up, source, line,
    edge_out, edge_in, carry_out, carry_in, wide, joined, local_out,
    load_sem, block_sem, store_sem, edge_send, edge_recv, carry_send, carry_recv,
):
    cells, equations, width = rhs.shape
    norm, surf = lax.axis_index("norm"), lax.axis_index("surf")
    norms, surfs = lax.axis_size("norm"), lax.axis_size("surf")
    has_below, has_above = norm > 0, norm < norms - 1
    has_left, has_right = surf > 0, surf < surfs - 1

    small = [
        pltpu.make_async_copy(src, dst, load_sem.at[i])
        for i, (src, dst) in enumerate(((prev_h, delta), (rhs_h, rhs), (diss_h, diss)))
    ]
    pairs = ((minus_h, minus), (plus_h, plus), (inv_h, inv), (low_h, low), (up_h, up))

    def block_copy(kind, cell):
        src, dst = pairs[kind]
        return pltpu.make_async_copy(src.at[cell], dst.at[cell], block_sem.at[kind, cell])

    for copy in small:
        copy.start()
    for cell in range(cells):
        for kind in range(3):
            block_copy(kind, cell).start()
    for cell in range(cells):
        block_copy(3, cell).start()
    for cell in reversed(range(cells)):
        block_copy(4, cell).start()

    neighbours = (
        (has_below, {"norm": norm - 1}),
        (has_above, {"norm": norm + 1}),
        (has_left, {"surf": surf - 1}),
        (has_right, {"surf": surf + 1}),
    )
    barrier = pltpu.get_barrier_semaphore()
    for present, where in neighbours:
        @pl.when(present)
        def _():
            pl.semaphore_signal(
                barrier, inc=1, device_id=where, device_id_type=pl.DeviceIdType.MESH
            )

    @pl.when(jnp.logical_not(has_left))
    def _():
        edge_in[:, 0] = jnp.zeros_like(edge_in[:, 0])

    @pl.when(jnp.logical_not(has_right))
    def _():
        edge_in[:, 1] = jnp.zeros_like(edge_in[:, 1])

    pl.semaphore_wait(barrier, sum(present.astype(jnp.int32) for present, _ in neighbours))

    def edge_copy(sweep, side, cell):
        return pltpu.make_async_remote_copy(
            src_ref=edge_out.at[sweep, cell],
            dst_ref=edge_in.at[sweep, side, cell],
            send_sem=edge_send.at[sweep, side, cell],
            recv_sem=edge_recv.at[sweep, side, cell],
            device_id={"surf": surf + 1 - 2 * side},
            device_id_type=pl.DeviceIdType.MESH,
        )

    def carry_copy(index, chunk):
        rows = pl.ds(chunk * CHUNK, CHUNK)
        return pltpu.make_async_remote_copy(
            src_ref=carry_out.at[index, rows],
            dst_ref=carry_in.at[index, rows],
            send_sem=carry_send.at[index, chunk],
            recv_sem=carry_recv.at[index, chunk],
            device_id={"norm": norm + 1 - 2 * (index % 2)},
            device_id_type=pl.DeviceIdType.MESH,
        )

    def widen(kind):
        def rows(step, _):
            cell, group = step // (equations // ROWS), step % (equations // ROWS)
            for a in range(ROWS):
                row = group * ROWS + a
                wide[kind - 3, cell, row] = pairs[kind][1][cell, row].astype(F32)
            return 0

        for cell in range(cells):
            block_copy(kind, cell).wait()
        lax.fori_loop(0, cells * (equations // ROWS), rows, 0)

    def join(unit, _):
        kind, step = unit // (cells - 1), unit % (cells - 1)
        cell = (step + 1) * (1 - kind) + (cells - 2 - step) * kind
        made, used = step % 2, (step + 1) % 2

        @pl.when(step == 0)
        def _():
            def copy_row(row, _):
                joined[kind, 1, row] = wide[kind, (cells - 1) * kind, row]
                return 0

            lax.fori_loop(0, equations, copy_row, 0)

        def rows(group, _):
            tile = pl.ds(group * TILE, TILE)
            total = jnp.zeros((TILE, equations, width), F32)
            for b in range(equations):
                total += wide[kind, cell, tile, b : b + 1, :] * joined[kind, used, b][None]
            joined[kind, made, tile] = total
            return 0

        lax.fori_loop(0, equations // TILE, rows, 0)
        return 0

    units = 2 * (cells - 1) * jnp.logical_and(has_below, has_above).astype(jnp.int32)
    done_0 = jnp.minimum(units, jnp.maximum(0, (norm - 2) // 2))
    done_1 = jnp.minimum(units, done_0 + (norms - 1 - norm) * 7 // 10)
    done_2 = jnp.minimum(units, jnp.maximum(done_1 + norm * 7 // 10, cells - 1))

    def send_edges(sweep, cell, value):
        edge_out[sweep, cell] = pack_edges(value)

        @pl.when(has_right)
        def _():
            edge_copy(sweep, 0, cell).start()

        @pl.when(has_left)
        def _():
            edge_copy(sweep, 1, cell).start()

    lane = lax.broadcasted_iota(jnp.int32, (equations, width), 1)

    def source_cell(sweep, cell):
        @pl.when(has_left)
        def _():
            edge_copy(sweep, 0, cell).wait_recv()

        @pl.when(has_right)
        def _():
            edge_copy(sweep, 1, cell).wait_recv()

        if sweep == 0:
            for kind in range(3):
                block_copy(kind, cell).wait()
        centre = delta[cell]
        left = unpack_edges(edge_in[sweep, 0, cell], equations)
        right = unpack_edges(edge_in[sweep, 1, cell], equations)
        left_one = pltpu.roll(jnp.where(lane == width - 1, left, centre), 1, 1)
        left_two = pltpu.roll(jnp.where(lane >= width - 2, left, centre), 2, 1)
        right_one = pltpu.roll(jnp.where(lane == 0, right, centre), width - 1, 1)
        right_two = pltpu.roll(jnp.where(lane <= 1, right, centre), width - 2, 1)
        fourth = left_two - 4.0 * left_one + 6.0 * centre - 4.0 * right_one + right_two
        residual = rhs[cell] - diss[cell] * fourth
        residual = residual - matvec(minus, cell, left_one)
        residual = residual - matvec(plus, cell, right_one)
        source[cell] = matvec(inv, cell, residual)

    small[0].wait()

    def first_edges(cell, _):
        send_edges(0, cell, delta[cell])
        return 0

    lax.fori_loop(0, cells, first_edges, 0)
    small[1].wait()
    small[2].wait()

    for sweep in range(SWEEPS):
        last_sweep = sweep == SWEEPS - 1

        def source_step(step, _):
            source_cell(sweep, step if sweep == 0 else cells - 1 - step)
            return 0

        lax.fori_loop(0, cells, source_step, 0)

        def run_pass(index, arrives, leaves, blocks, given, result, finish):
            backward = index % 2
            place = lambda step: cells - 1 - step if backward else step

            @pl.when(arrives)
            def _():
                for chunk in range(equations // CHUNK):
                    carry_copy(index, chunk).wait_recv()

            @pl.when(jnp.logical_not(arrives))
            def _():
                first = given[place(0)]
                carry_in[index] = first
                result[place(0)] = first
                finish(place(0), first)

            def step_cell(step, carry):
                cell = place(step)
                value = given[cell] + matvec(blocks, cell, carry)
                result[cell] = value
                finish(cell, value)
                return value

            begin = 1 - arrives.astype(jnp.int32)
            carry = lax.fori_loop(begin, cells - 1, step_cell, carry_in[index])
            last = place(cells - 1)

            @pl.when(leaves)
            def _():
                def send_group(group, sums):
                    rows = slice(group * ROWS, (group + 1) * ROWS)
                    carry_out[index, rows] = given[last, rows] + sums
                    if (group + 1) * ROWS % CHUNK == 0:
                        carry_copy(index, group * ROWS // CHUNK).start()

                matvec(blocks, last, carry, send_group)
                value = carry_out[index]
                result[last] = value
                finish(last, value)

            @pl.when(jnp.logical_not(leaves))
            def _():
                value = given[last] + matvec(blocks, last, carry)
                result[last] = value
                finish(last, value)

        def run_joined(index, arrives, leaves, blocks, given, result, finish):
            backward = index % 2
            place = lambda step: cells - 1 - step if backward else step
            middle = jnp.logical_and(arrives, leaves)
            last = place(cells - 1)

            @pl.when(middle)
            def _():
                def local_step(step, carry):
                    cell = place(step)
                    return given[cell] + matvec(blocks, cell, carry)

                local_out[...] = lax.fori_loop(1, cells, local_step, given[place(0)])
                for chunk in range(equations // CHUNK):
                    carry_copy(index, chunk).wait_recv()

                def send_group(group, sums):
                    rows = slice(group * ROWS, (group + 1) * ROWS)
                    carry_out[index, rows] = local_out[rows] + sums
                    if (group + 1) * ROWS % CHUNK == 0:
                        carry_copy(index, group * ROWS // CHUNK).start()

                matvec(joined.at[backward], cells % 2, carry_in[index], send_group)

                def step_cell(step, carry):
                    cell = place(step)
                    value = given[cell] + matvec(blocks, cell, carry)
                    result[cell] = value
                    finish(cell, value)
                    return value

                lax.fori_loop(0, cells - 1, step_cell, carry_in[index])
                value = carry_out[index]
                result[last] = value
                finish(last, value)

            @pl.when(jnp.logical_not(middle))
            def _():
                run_pass(index, arrives, leaves, blocks, given, result, finish)

        def keep(cell, value):
            pass

        def pass_on(cell, value):
            if last_sweep:
                pltpu.make_async_copy(delta.at[cell], out_h.at[cell], store_sem.at[cell]).start()
            else:
                send_edges(sweep + 1, cell, value)

        if sweep == 0:
            widen(3)

            @pl.when(has_below)
            def _():
                widen(4)

            lax.fori_loop(0, done_0, join, 0)

        run = run_pass if sweep == 0 else run_joined
        if sweep == 1:
            lax.fori_loop(done_1, done_2, join, 0)
        run(2 * sweep, has_below, has_above, wide.at[0], source, line, keep)
        if sweep == 0:
            @pl.when(jnp.logical_not(has_below))
            def _():
                widen(4)

            lax.fori_loop(done_0, done_1, join, 0)
        else:
            lax.fori_loop(done_2, units, join, 0)

        run(2 * sweep + 1, has_above, has_below, wide.at[1], line, delta, pass_on)

    for cell in range(cells):
        pltpu.make_async_copy(delta.at[cell], out_h.at[cell], store_sem.at[cell]).wait()
    for sweep in range(SWEEPS):
        for cell in range(cells):
            for side, present in ((0, has_right), (1, has_left)):
                @pl.when(present)
                def _():
                    edge_copy(sweep, side, cell).wait_send()

        for index, leaves in ((2 * sweep, has_above), (2 * sweep + 1, has_below)):
            @pl.when(leaves)
            def _():
                for chunk in range(equations // CHUNK):
                    carry_copy(index, chunk).wait_send()


def shards(*arrays):
    cells, equations, width = arrays[0].shape
    vector = pltpu.VMEM((cells, equations, width), F32)
    matrix = pltpu.VMEM((cells, equations, equations, width), jnp.bfloat16)
    dma = pltpu.SemaphoreType.DMA
    return pl.pallas_call(
        kernel,
        out_shape=jax.ShapeDtypeStruct((cells, equations, width), F32),
        in_specs=[pl.BlockSpec(memory_space=pl.ANY)] * len(arrays),
        out_specs=pl.BlockSpec(memory_space=pl.ANY),
        scratch_shapes=[
            vector, vector, matrix, matrix, vector, matrix, matrix, matrix, vector, vector,
            pltpu.VMEM((SWEEPS, cells, ROWS, width), F32),
            pltpu.VMEM((SWEEPS, 2, cells, ROWS, width), F32),
            pltpu.VMEM((2 * SWEEPS, equations, width), F32),
            pltpu.VMEM((2 * SWEEPS, equations, width), F32),
            pltpu.VMEM((2, cells, equations, equations, width), F32),
            pltpu.VMEM((2, 2, equations, equations, width), F32),
            pltpu.VMEM((equations, width), F32),
            dma((3,)), dma((5, cells)), dma((cells,)),
            dma((SWEEPS, 2, cells)), dma((SWEEPS, 2, cells)),
            dma((2 * SWEEPS, equations // CHUNK)), dma((2 * SWEEPS, equations // CHUNK)),
        ],
        compiler_params=pltpu.CompilerParams(
            collective_id=0, has_side_effects=True, vmem_limit_bytes=56 * 1024 * 1024
        ),
        name="line_relaxation",
    )(*arrays)


def solution(mesh):
    vectors = P("norm", None, "surf")
    blocks = P("norm", None, None, "surf")
    return jax.shard_map(
        shards,
        mesh=mesh,
        in_specs=(vectors, vectors, blocks, blocks, vectors, blocks, blocks, blocks),
        out_specs=vectors,
        check_vma=False,
    )
```

```python
import functools

import jax
import jax.numpy as jnp
from jax import lax
from jax.experimental import pallas as pl
from jax.experimental.pallas import tpu as pltpu
from jax.sharding import PartitionSpec as P

SWEEPS = 2
ROWS = 8
EDGE = 2
CHUNK = 24
TILE = 4
F32 = jnp.float32


def row_sums(regs):
    row = lax.broadcasted_iota(jnp.int32, regs[0].shape, 0)
    for half in (4, 2, 1):
        low = (row % (2 * half)) < half
        merged = []
        for i in range(half):
            a, b = regs[i], regs[i + half]
            keep = jnp.where(low, a, b)
            move = jnp.where(low, b, a)
            if half == 4:
                moved = pltpu.roll(move, half, 0)
            else:
                moved = jnp.where(
                    low, pltpu.roll(move, ROWS - half, 0), pltpu.roll(move, half, 0)
                )
            merged.append(keep + moved)
        regs = merged
    return regs[0]


def matvec(block_ref, cell, vector, each_group=None):
    equations = vector.shape[0]
    out = []
    for group in range(equations // ROWS):
        regs = []
        for a in range(ROWS):
            product = block_ref[cell, group * ROWS + a].astype(F32) * vector
            parts = [product[i : i + ROWS] for i in range(0, equations, ROWS)]
            while len(parts) > 1:
                parts = [
                    parts[i] + parts[i + 1] if i + 1 < len(parts) else parts[i]
                    for i in range(0, len(parts), 2)
                ]
            regs.append(parts[0])
        out.append(row_sums(regs))
        if each_group is not None:
            each_group(group, out[-1])
    return jnp.concatenate(out, axis=0)


def pack_edges(cell):
    equations, width = cell.shape
    lane = lax.broadcasted_iota(jnp.int32, (ROWS, width), 1)
    packed = jnp.zeros((ROWS, width), F32)
    for g in range(equations // ROWS):
        moved = pltpu.roll(cell[g * ROWS : (g + 1) * ROWS], EDGE + 2 * EDGE * g, 1)
        packed = jnp.where(lane // (2 * EDGE) == g, moved, packed)
    return packed


def unpack_edges(packed, equations):
    width = packed.shape[1]
    return jnp.concatenate(
        [
            pltpu.roll(packed, width - EDGE - 2 * EDGE * g, 1)
            for g in range(equations // ROWS)
        ],
        axis=0,
    )


def kernel(
    rhs_h, prev_h, minus_h, plus_h, diss_h, inv_h, low_h, up_h, out_h,
    rhs, delta, minus, plus, diss, inv, low, up, source, line,
    edge_out, edge_in, carry_out, carry_in, wide, joined, local_out,
    load_sem, block_sem, store_sem, edge_send, edge_recv, carry_send, carry_recv,
):
    cells, equations, width = rhs.shape
    norm, surf = lax.axis_index("norm"), lax.axis_index("surf")
    norms, surfs = lax.axis_size("norm"), lax.axis_size("surf")
    has_below, has_above = norm > 0, norm < norms - 1
    has_left, has_right = surf > 0, surf < surfs - 1

    small = [
        pltpu.make_async_copy(src, dst, load_sem.at[i])
        for i, (src, dst) in enumerate(((prev_h, delta), (rhs_h, rhs), (diss_h, diss)))
    ]
    pairs = ((minus_h, minus), (plus_h, plus), (inv_h, inv), (low_h, low), (up_h, up))

    def block_copy(kind, cell):
        src, dst = pairs[kind]
        return pltpu.make_async_copy(src.at[cell], dst.at[cell], block_sem.at[kind, cell])

    for copy in small:
        copy.start()
    for cell in range(cells):
        for kind in range(3):
            block_copy(kind, cell).start()
    for cell in range(cells):
        block_copy(3, cell).start()
    for cell in reversed(range(cells)):
        block_copy(4, cell).start()

    neighbours = (
        (has_below, {"norm": norm - 1}),
        (has_above, {"norm": norm + 1}),
        (has_left, {"surf": surf - 1}),
        (has_right, {"surf": surf + 1}),
    )
    barrier = pltpu.get_barrier_semaphore()
    for present, where in neighbours:
        @pl.when(present)
        def _():
            pl.semaphore_signal(
                barrier, inc=1, device_id=where, device_id_type=pl.DeviceIdType.MESH
            )

    @pl.when(jnp.logical_not(has_left))
    def _():
        edge_in[:, 0] = jnp.zeros_like(edge_in[:, 0])

    @pl.when(jnp.logical_not(has_right))
    def _():
        edge_in[:, 1] = jnp.zeros_like(edge_in[:, 1])

    pl.semaphore_wait(barrier, sum(present.astype(jnp.int32) for present, _ in neighbours))

    def edge_copy(sweep, side, cell):
        return pltpu.make_async_remote_copy(
            src_ref=edge_out.at[sweep, cell],
            dst_ref=edge_in.at[sweep, side, cell],
            send_sem=edge_send.at[sweep, side, cell],
            recv_sem=edge_recv.at[sweep, side, cell],
            device_id={"surf": surf + 1 - 2 * side},
            device_id_type=pl.DeviceIdType.MESH,
        )

    def carry_copy(index, chunk):
        rows = pl.ds(chunk * CHUNK, CHUNK)
        return pltpu.make_async_remote_copy(
            src_ref=carry_out.at[index, rows],
            dst_ref=carry_in.at[index, rows],
            send_sem=carry_send.at[index, chunk],
            recv_sem=carry_recv.at[index, chunk],
            device_id={"norm": norm + 1 - 2 * (index % 2)},
            device_id_type=pl.DeviceIdType.MESH,
        )

    def widen(kind):
        def rows(step, _):
            cell, group = step // (equations // ROWS), step % (equations // ROWS)
            for a in range(ROWS):
                row = group * ROWS + a
                wide[kind - 3, cell, row] = pairs[kind][1][cell, row].astype(F32)
            return 0

        for cell in range(cells):
            block_copy(kind, cell).wait()
        lax.fori_loop(0, cells * (equations // ROWS), rows, 0)

    def join(unit, _):
        kind, step = unit // (cells - 1), unit % (cells - 1)
        cell = (step + 1) * (1 - kind) + (cells - 2 - step) * kind
        made, used = step % 2, (step + 1) % 2

        @pl.when(step == 0)
        def _():
            def copy_row(row, _):
                joined[kind, 1, row] = wide[kind, (cells - 1) * kind, row]
                return 0

            lax.fori_loop(0, equations, copy_row, 0)

        def rows(group, _):
            tile = pl.ds(group * TILE, TILE)
            total = jnp.zeros((TILE, equations, width), F32)
            for b in range(equations):
                total += wide[kind, cell, tile, b : b + 1, :] * joined[kind, used, b][None]
            joined[kind, made, tile] = total
            return 0

        lax.fori_loop(0, equations // TILE, rows, 0)
        return 0

    units = 2 * (cells - 1) * jnp.logical_and(has_below, has_above).astype(jnp.int32)
    done_0 = jnp.minimum(units, jnp.maximum(0, (norm - 2) // 2))
    done_1 = jnp.minimum(units, done_0 + (norms - 1 - norm) * 7 // 10)
    done_2 = jnp.minimum(units, jnp.maximum(done_1 + norm * 7 // 10, cells - 1))

    def send_edges(sweep, cell, value):
        edge_out[sweep, cell] = pack_edges(value)

        @pl.when(has_right)
        def _():
            edge_copy(sweep, 0, cell).start()

        @pl.when(has_left)
        def _():
            edge_copy(sweep, 1, cell).start()

    lane = lax.broadcasted_iota(jnp.int32, (equations, width), 1)

    def source_cell(sweep, cell):
        @pl.when(has_left)
        def _():
            edge_copy(sweep, 0, cell).wait_recv()

        @pl.when(has_right)
        def _():
            edge_copy(sweep, 1, cell).wait_recv()

        if sweep == 0:
            for kind in range(3):
                block_copy(kind, cell).wait()
        centre = delta[cell]
        left = unpack_edges(edge_in[sweep, 0, cell], equations)
        right = unpack_edges(edge_in[sweep, 1, cell], equations)
        left_one = pltpu.roll(jnp.where(lane == width - 1, left, centre), 1, 1)
        left_two = pltpu.roll(jnp.where(lane >= width - 2, left, centre), 2, 1)
        right_one = pltpu.roll(jnp.where(lane == 0, right, centre), width - 1, 1)
        right_two = pltpu.roll(jnp.where(lane <= 1, right, centre), width - 2, 1)
        fourth = left_two - 4.0 * left_one + 6.0 * centre - 4.0 * right_one + right_two
        residual = rhs[cell] - diss[cell] * fourth
        residual = residual - matvec(minus, cell, left_one)
        residual = residual - matvec(plus, cell, right_one)
        source[cell] = matvec(inv, cell, residual)

    small[0].wait()

    def first_edges(cell, _):
        send_edges(0, cell, delta[cell])
        return 0

    lax.fori_loop(0, cells, first_edges, 0)
    small[1].wait()
    small[2].wait()

    for sweep in range(SWEEPS):
        last_sweep = sweep == SWEEPS - 1

        def source_step(step, _):
            source_cell(sweep, step if sweep == 0 else cells - 1 - step)
            return 0

        lax.fori_loop(0, cells, source_step, 0)

        def run_pass(index, arrives, leaves, blocks, given, result, finish):
            backward = index % 2
            place = lambda step: cells - 1 - step if backward else step

            @pl.when(arrives)
            def _():
                for chunk in range(equations // CHUNK):
                    carry_copy(index, chunk).wait_recv()

            @pl.when(jnp.logical_not(arrives))
            def _():
                first = given[place(0)]
                carry_in[index] = first
                result[place(0)] = first
                finish(place(0), first)

            def step_cell(step, carry):
                cell = place(step)
                value = given[cell] + matvec(blocks, cell, carry)
                result[cell] = value
                finish(cell, value)
                return value

            begin = 1 - arrives.astype(jnp.int32)
            carry = lax.fori_loop(begin, cells - 1, step_cell, carry_in[index])
            last = place(cells - 1)

            @pl.when(leaves)
            def _():
                def send_group(group, sums):
                    rows = slice(group * ROWS, (group + 1) * ROWS)
                    carry_out[index, rows] = given[last, rows] + sums
                    if (group + 1) * ROWS % CHUNK == 0:
                        carry_copy(index, group * ROWS // CHUNK).start()

                matvec(blocks, last, carry, send_group)
                value = carry_out[index]
                result[last] = value
                finish(last, value)

            @pl.when(jnp.logical_not(leaves))
            def _():
                value = given[last] + matvec(blocks, last, carry)
                result[last] = value
                finish(last, value)

        def run_joined(index, arrives, leaves, blocks, given, result, finish):
            backward = index % 2
            place = lambda step: cells - 1 - step if backward else step
            middle = jnp.logical_and(arrives, leaves)
            last = place(cells - 1)

            @pl.when(middle)
            def _():
                def local_step(step, carry):
                    cell = place(step)
                    return given[cell] + matvec(blocks, cell, carry)

                local_out[...] = lax.fori_loop(1, cells, local_step, given[place(0)])
                for chunk in range(equations // CHUNK):
                    carry_copy(index, chunk).wait_recv()

                def send_group(group, sums):
                    rows = slice(group * ROWS, (group + 1) * ROWS)
                    carry_out[index, rows] = local_out[rows] + sums
                    if (group + 1) * ROWS % CHUNK == 0:
                        carry_copy(index, group * ROWS // CHUNK).start()

                matvec(joined.at[backward], cells % 2, carry_in[index], send_group)

                def step_cell(step, carry):
                    cell = place(step)
                    value = given[cell] + matvec(blocks, cell, carry)
                    result[cell] = value
                    finish(cell, value)
                    return value

                lax.fori_loop(0, cells - 1, step_cell, carry_in[index])
                value = carry_out[index]
                result[last] = value
                finish(last, value)

            @pl.when(jnp.logical_not(middle))
            def _():
                run_pass(index, arrives, leaves, blocks, given, result, finish)

        def keep(cell, value):
            pass

        def pass_on(cell, value):
            if last_sweep:
                pltpu.make_async_copy(delta.at[cell], out_h.at[cell], store_sem.at[cell]).start()
            else:
                send_edges(sweep + 1, cell, value)

        if sweep == 0:
            widen(3)

            @pl.when(has_below)
            def _():
                widen(4)

            lax.fori_loop(0, done_0, join, 0)

        run = run_pass if sweep == 0 else run_joined
        if sweep == 1:
            lax.fori_loop(done_1, done_2, join, 0)
        run(2 * sweep, has_below, has_above, wide.at[0], source, line, keep)
        if sweep == 0:
            @pl.when(jnp.logical_not(has_below))
            def _():
                widen(4)

            lax.fori_loop(done_0, done_1, join, 0)
        else:
            lax.fori_loop(done_2, units, join, 0)

        run(2 * sweep + 1, has_above, has_below, wide.at[1], line, delta, pass_on)

    for cell in range(cells):
        pltpu.make_async_copy(delta.at[cell], out_h.at[cell], store_sem.at[cell]).wait()
    for sweep in range(SWEEPS):
        for cell in range(cells):
            for side, present in ((0, has_right), (1, has_left)):
                @pl.when(present)
                def _():
                    edge_copy(sweep, side, cell).wait_send()

        for index, leaves in ((2 * sweep, has_above), (2 * sweep + 1, has_below)):
            @pl.when(leaves)
            def _():
                for chunk in range(equations // CHUNK):
                    carry_copy(index, chunk).wait_send()


def shards(*arrays):
    cells, equations, width = arrays[0].shape
    vector = pltpu.VMEM((cells, equations, width), F32)
    matrix = pltpu.VMEM((cells, equations, equations, width), jnp.bfloat16)
    dma = pltpu.SemaphoreType.DMA
    return pl.pallas_call(
        kernel,
        out_shape=jax.ShapeDtypeStruct((cells, equations, width), F32),
        in_specs=[pl.BlockSpec(memory_space=pl.ANY)] * len(arrays),
        out_specs=pl.BlockSpec(memory_space=pl.ANY),
        scratch_shapes=[
            vector, vector, matrix, matrix, vector, matrix, matrix, matrix, vector, vector,
            pltpu.VMEM((SWEEPS, cells, ROWS, width), F32),
            pltpu.VMEM((SWEEPS, 2, cells, ROWS, width), F32),
            pltpu.VMEM((2 * SWEEPS, equations, width), F32),
            pltpu.VMEM((2 * SWEEPS, equations, width), F32),
            pltpu.VMEM((2, cells, equations, equations, width), F32),
            pltpu.VMEM((2, 2, equations, equations, width), F32),
            pltpu.VMEM((equations, width), F32),
            dma((3,)), dma((5, cells)), dma((cells,)),
            dma((SWEEPS, 2, cells)), dma((SWEEPS, 2, cells)),
            dma((2 * SWEEPS, equations // CHUNK)), dma((2 * SWEEPS, equations // CHUNK)),
        ],
        compiler_params=pltpu.CompilerParams(
            collective_id=0, has_side_effects=True, vmem_limit_bytes=56 * 1024 * 1024
        ),
        name="line_relaxation",
    )(*arrays)


def solution(mesh):
    vectors = P("norm", None, "surf")
    blocks = P("norm", None, None, "surf")
    return jax.shard_map(
        shards,
        mesh=mesh,
        in_specs=(vectors, vectors, blocks, blocks, vectors, blocks, blocks, blocks),
        out_specs=vectors,
        check_vma=False,
    )
```
